512 devices in a mesh: dp: 32 (over z_lo, y, core), ctx: 16 (over x, z_hi).
Axes of the slice: x: 4, y: 4, z: 16 (z_hi: 4, z_lo: 4; z = z_hi * 4 + z_lo), core: 2. Of those that a mesh axis runs over, the one named last changes fastest.
Arguments:
- queries: bfloat16 [32, 128, 2560], P('dp', 'ctx'), may hold values from -5.5 to 5.5
- query_tangent: bfloat16 [32, 128, 2560], P('dp', 'ctx'), may hold values from -6 to 6
- keys: bfloat16 [32, 2304, 2560], P('dp', 'ctx'), may hold values from -5.5 to 5.5
- values: bfloat16 [32, 2304, 2560], P('dp', 'ctx'), may hold values from -6 to 6
- key_tangent: bfloat16 [32, 2304, 2560], P('dp', 'ctx'), may hold values from -6 to 6
- value_tangent: bfloat16 [32, 2304, 2560], P('dp', 'ctx'), may hold values from -6 to 6
- velocity: bfloat16 [32, 128, 2560], P('dp', 'ctx'), may hold values from -6 to 6
- out_weight: bfloat16 [2560, 2560], P('dp', 'ctx'), may hold values from -0.125 to 0.125
- pair_index: int32 [32, 2], P('dp'), may hold values from 0 to 14
Outputs:
- grad_queries: bfloat16 [32, 128, 2560], P('dp', 'ctx')
- grad_keys: bfloat16 [32, 2304, 2560], P('dp', 'ctx')
- grad_values: bfloat16 [32, 2304, 2560], P('dp', 'ctx')
The draws below stay inside these ranges and needn't reach their ends.
All inputs are finite; a program needn't handle non-finite values.
Results may differ from the reference program's by a relative error of at most 0.029.
Values may be sent and summed in bfloat16 or wider, within the bound.
A program may use at most 64 MiB of HBM per device.

```python
import jax
import jax.numpy as jnp
from jax import lax

HEADS = 20
HDIM = 128
DO = 2560
KV_DEV = 144
HD = 2560
CLIPS = 32
QTOK = 128
CLIP = 2304
N_CTX = 16


def draw_queries(key, part):
    key = jax.random.fold_in(key, 3)
    field = jnp.clip(jax.random.normal(key, (CLIPS, QTOK, HD), jnp.float32), -5.5, 5.5)
    return field.astype(jnp.bfloat16)


def draw_keys(key, part):
    key = jax.random.fold_in(key, 5)
    field = jnp.clip(jax.random.normal(key, (CLIPS, CLIP, HD), jnp.float32), -5.5, 5.5)
    return field.astype(jnp.bfloat16)


def touch_ends(drawn, rng, low, largest):
    shape = drawn.shape
    spot = [jax.random.randint(jax.random.fold_in(rng, axis), (), 0, shape[axis]) for axis in range(len(shape))]
    drawn = drawn.at[tuple(spot)].set(low)
    longest = shape.index(max(shape))
    spot[longest] = (spot[longest] + 1) % shape[longest]
    return drawn.at[tuple(spot)].set(largest)


def levels(key, dims, cuts, least, largest):
    level, own = 1.0, jax.random.fold_in(key, 6)
    for dim, parts in cuts:
        draws = jnp.exp(jax.random.uniform(jax.random.fold_in(own, dim), (parts,), jnp.float32, least / len(cuts), largest / len(cuts)))
        level = level * jnp.repeat(draws, dims[dim] // parts).reshape([-1 if axis == dim else 1 for axis in range(len(dims))])
    return level


def scatter_about(stream_key, shape, scale, reach, shards=(), kind=jnp.bfloat16):
    drawn = scale * jax.random.normal(stream_key, shape, jnp.float32)
    if shards:
        drawn = drawn * levels(stream_key, shape, shards, -0.22, 0.18)
    return jnp.clip(drawn, -reach, reach).astype(kind)


def setup_inputs(seed: int = 0) -> dict:
    splits = jax.random.split(jax.random.key(seed), 10)
    return {
        "queries": draw_queries(jax.random.fold_in(splits[9], 71), 0),
        "query_tangent": scatter_about(splits[1], (CLIPS, QTOK, HD), 1.0, 6.0, ((0, 32), (1, 16))),
        "keys": draw_keys(jax.random.fold_in(splits[9], 71), 0),
        "values": scatter_about(splits[3], (CLIPS, CLIP, HD), 1.0, 6.0, ((0, 32), (1, 16))),
        "key_tangent": scatter_about(splits[4], (CLIPS, CLIP, HD), 1.0, 6.0, ((0, 32), (1, 16))),
        "value_tangent": scatter_about(splits[5], (CLIPS, CLIP, HD), 1.0, 6.0, ((0, 32), (1, 16))),
        "velocity": scatter_about(splits[6], (CLIPS, QTOK, DO), 1.0, 6.0, ((0, 32), (1, 16))),
        "out_weight": scatter_about(splits[7], (HD, DO), HD ** -0.5, 0.125, ((0, 32), (1, 16))),
        "pair_index": touch_ends(jax.random.randint(splits[8], (CLIPS, 2), 0, 15), jax.random.fold_in(splits[8], 1), 0, 14).astype(jnp.int32),
    }


time_grid = 15.0


def rounded(x):
    return lax.optimization_barrier(x.astype(jnp.bfloat16)).astype(jnp.float32)


def clip_step(items, out_weight):
    queries, query_tangent, keys, values, key_tangent, value_tangent, velocity, pair = items
    scale = HDIM ** -0.5
    qf = queries.astype(jnp.float32).reshape(QTOK, HEADS, HDIM)
    qtf = query_tangent.astype(jnp.float32).reshape(QTOK, HEADS, HDIM)
    blocks = (N_CTX, KV_DEV, HEADS, HDIM)
    kf = keys.astype(jnp.float32).reshape(blocks)
    vf = values.astype(jnp.float32).reshape(blocks)
    ktf = key_tangent.astype(jnp.float32).reshape(blocks)
    vtf = value_tangent.astype(jnp.float32).reshape(blocks)
    score = jnp.einsum('qhd,jkhd->jhqk', qf, kf) * scale
    slope = (jnp.einsum('qhd,jkhd->jhqk', qtf, kf) + jnp.einsum('qhd,jkhd->jhqk', qf, ktf)) * scale
    peak = jnp.max(score, axis=-1)
    expd = jnp.exp(score - peak[..., None])
    total = jnp.sum(expd, axis=-1)
    bend = jnp.sum(expd * slope, axis=-1)
    expd_b = rounded(expd)
    mixed_b = rounded(expd * slope)
    part_a = rounded(jnp.einsum('jhqk,jkhd->jqhd', expd_b, vf))
    part_c = rounded(jnp.einsum('jhqk,jkhd->jqhd', mixed_b, vf) + jnp.einsum('jhqk,jkhd->jqhd', expd_b, vtf))
    top = jnp.max(peak, axis=0)
    weights = jnp.exp(peak - top[None])
    norm = jnp.sum(weights * total, axis=0)
    bent = jnp.sum(weights * bend, axis=0)
    weight_q = jnp.transpose(weights, (0, 2, 1))[..., None]
    numer = jnp.sum(weight_q * part_a, axis=0)
    tang = jnp.sum(weight_q * part_c, axis=0)
    norm_q = norm.T[..., None]
    attended = numer / norm_q
    attended_t = tang / norm_q - (bent.T / norm.T)[..., None] * attended
    high = jnp.max(pair)
    low = jnp.min(pair)
    gap = (high + 1 - low).astype(jnp.float32) / time_grid
    out_b = attended.reshape(QTOK, HD).astype(jnp.bfloat16)
    scaled_t = (gap * attended_t).reshape(QTOK, HD).astype(jnp.bfloat16)
    direct = jnp.dot(out_b, out_weight, preferred_element_type=jnp.float32)
    slope_out = jnp.dot(scaled_t, out_weight, preferred_element_type=jnp.float32)
    err = direct - (velocity.astype(jnp.float32) - slope_out)
    grad_u = err.astype(jnp.bfloat16)
    grad_o = jnp.dot(grad_u, out_weight.T, preferred_element_type=jnp.float32).astype(jnp.bfloat16)
    gof = grad_o.astype(jnp.float32).reshape(QTOK, HEADS, HDIM)
    delta = jnp.sum(gof * attended, axis=-1)
    prob = jnp.exp(score - top[None, :, :, None]) / norm[None, :, :, None]
    prob_b = rounded(prob)
    grad_values = jnp.einsum('jhqk,qhd->jkhd', prob_b, gof).astype(jnp.bfloat16)
    dprob = jnp.einsum('qhd,jkhd->jhqk', gof, vf)
    dscore = prob * (dprob - delta.T[None, :, :, None]) * scale
    ds_b = rounded(dscore)
    grad_keys = jnp.einsum('jhqk,qhd->jkhd', ds_b, qf).astype(jnp.bfloat16)
    parts_q = rounded(jnp.einsum('jhqk,jkhd->jqhd', ds_b, kf))
    grad_queries = jnp.sum(parts_q, axis=0).astype(jnp.bfloat16)
    return (grad_queries.reshape(QTOK, HD), grad_keys.reshape(CLIP, HD), grad_values.reshape(CLIP, HD))


def reference(queries, query_tangent, keys, values, key_tangent, value_tangent, velocity, out_weight, pair_index):
    items = (queries, query_tangent, keys, values, key_tangent, value_tangent, velocity, pair_index)
    grad_queries, grad_keys, grad_values = lax.map(lambda one: clip_step(one, out_weight), items)
    return (grad_queries, grad_keys, grad_values)
```

```python
import jax
import jax.numpy as jnp
from jax import lax
from jax.experimental import pallas as pl
from jax.experimental.pallas import tpu as pltpu
from jax.sharding import PartitionSpec as P

HEADS = 20
HDIM = 128
GROUP = 5
PER_STEP = 2
COPIES = 112
time_grid = 15.0

F32 = jnp.float32
BF16 = jnp.bfloat16
MESH = pl.DeviceIdType.MESH
NT = (((1,), (1,)), ((), ()))
TN = (((0,), (0,)), ((), ()))
NN = (((1,), (0,)), ((), ()))


def mm(a, b, dims):
    return lax.dot_general(a, b, dims, preferred_element_type=F32)


class Net:
    def __init__(self, send, recv):
        self.send, self.recv, self.used, self.all = send, recv, 0, []

    def copy(self, src, dst, device):
        n = self.used
        self.used += 1
        c = pltpu.make_async_remote_copy(
            src_ref=src,
            dst_ref=dst,
            send_sem=self.send.at[n],
            recv_sem=self.recv.at[n],
            device_id=device,
            device_id_type=MESH,
        )
        c.start()
        self.all.append(c)
        return c


class Ring:
    def __init__(self, net, p, name, device):
        self.net, self.p = net, p
        self.right, self.left, self.far = [lax.rem(p + k, 4) for k in (1, 3, 2)]
        self.to = lambda q: {name: device(q)}

    def gather(self, buf, half):
        p, r, l = self.p, self.right, self.left
        at = lambda b, k: half(buf, b, k)
        go = lambda b, k, q: self.net.copy(at(b, k), at(b, k), self.to(q))
        a = go(p, 0, r)
        b = go(p, 1, l)
        c = go(p, 1, r)
        d = go(p, 0, l)

        def finish():
            a.wait_recv()
            e = go(l, 0, r)
            b.wait_recv()
            f = go(r, 1, l)
            for x in (c, d, e, f):
                x.wait_recv()

        return finish

    def scatter(self, buf, half, tmp, got_l, got_r, half1):
        p, r, l, o = self.p, self.right, self.left, self.far
        to_r, to_l = self.to(r), self.to(l)
        a = self.net.copy(half(buf, o, 0), tmp.at[0], to_r)
        b = self.net.copy(half(buf, o, 1), tmp.at[1], to_l)
        c = self.net.copy(half(buf, r, 1), half1(got_l, 1), to_r)
        d = self.net.copy(half(buf, l, 0), half1(got_r, 0), to_l)
        a.wait_recv()
        x = half(buf, r, 0)
        x[...] = (x[...].astype(F32) + tmp[0].astype(F32)).astype(BF16)
        e = self.net.copy(x, half1(got_l, 0), to_r)
        b.wait_recv()
        y = half(buf, l, 1)
        y[...] = (y[...].astype(F32) + tmp[1].astype(F32)).astype(BF16)
        f = self.net.copy(y, half1(got_r, 1), to_l)
        for w in (c, d, e, f):
            w.wait_recv()

    def exchange(self, src, dst):
        cs = [self.net.copy(src(q), dst, self.to(q)) for q in (self.right, self.left, self.far)]

        def finish():
            for c in cs:
                c.wait_recv()

        return finish


def rows_half(n):
    return lambda buf, b, k: buf.at[b, pl.ds(k * n, n)]


def rows_half1(n):
    return lambda buf, k: buf.at[pl.ds(k * n, n)]


def kernel(
    q_in, qt_in, vel_in, pair, k_hbm, v_hbm, kt_hbm, vt_hbm, w_hbm,
    gq_out, dk_hbm, dv_hbm,
    k_, v_, kt_, vt_, w_, dk_, dv_,
    qz, qx, vsrc, vz, vx, sc, sl,
    st, st_x, st_z, lm, dl, dl_x, dl_z, dm,
    s_c, s_tx, s_lx, s_rx, s_z, s_tz, s_lz, s_rz, s_full,
    g_c, g_tx, g_lx, g_rx, g_z, g_tz, g_lz, g_rz, g_full,
    a_c, a_tx, a_lx, a_rx, a_z, a_tz, a_lz, a_rz,
    load_sem, store_sem, send_sem, recv_sem,
):
    scale = HDIM ** (-0.5)
    ctx = lax.axis_index("ctx")
    dp = lax.axis_index("dp")
    x, zh = lax.div(ctx, 4), lax.rem(ctx, 4)
    zl, y, core = lax.div(dp, 8), lax.rem(lax.div(dp, 2), 4), lax.rem(dp, 2)

    net = Net(send_sem, recv_sem)
    ring_x = Ring(net, x, "ctx", lambda q: q * 4 + zh)
    ring_z = Ring(net, zh, "ctx", lambda q: x * 4 + q)
    ring_y = Ring(net, y, "dp", lambda q: zl * 8 + q * 2 + core)
    line_z = Ring(net, zl, "dp", lambda q: q * 8 + y * 2 + core)
    twin = {"dp": zl * 8 + y * 2 + (1 - core)}

    w_own = w_.at[zl, y, core]
    loads = [
        pltpu.make_async_copy(src, dst, load_sem.at[n])
        for n, (src, dst) in enumerate(
            [
                (w_hbm, w_own),
                (k_hbm.at[0], k_),
                (kt_hbm.at[0], kt_),
                (v_hbm.at[0], v_),
                (vt_hbm.at[0], vt_),
            ]
        )
    ]
    for c in loads:
        c.start()

    barrier = pltpu.get_barrier_semaphore()
    for ring in (ring_z, ring_x, ring_y, line_z):
        for pos in (ring.right, ring.left, ring.far):
            pl.semaphore_signal(barrier, inc=1, device_id=ring.to(pos), device_id_type=MESH)
    pl.semaphore_signal(barrier, inc=1, device_id=twin, device_id_type=MESH)

    qz[zh] = jnp.concatenate([q_in[0].astype(F32), qt_in[0].astype(F32)], axis=0).astype(BF16)
    vel = vel_in[0].astype(F32)
    for c in range(16):
        vsrc[c % 4, c // 4] = vel[:, c * 160 : (c + 1) * 160]
    high = jnp.maximum(pair[0, 0], pair[0, 1])
    low = jnp.minimum(pair[0, 0], pair[0, 1])
    gap = (high + 1 - low).astype(F32) / time_grid
    st[...] = jnp.ones_like(st)
    dl[...] = jnp.zeros_like(dl)
    pl.semaphore_wait(barrier, 13)

    q_done = ring_z.gather(qz, lambda buf, b, k: buf.at[b, :, pl.ds(k * 1280, 1280)])
    loads[0].wait()
    w_done = ring_y.exchange(lambda q: w_own, w_own)
    q_done()
    both = [qz[z].astype(F32) for z in range(4)]
    qx[x, 0] = jnp.concatenate([t[:8] for t in both], axis=0).astype(BF16)
    qx[x, 1] = jnp.concatenate([t[8:] for t in both], axis=0).astype(BF16)
    q_done = ring_x.gather(qx, lambda buf, b, k: buf.at[b, k])
    w_done()
    w_done = line_z.exchange(lambda q: w_.at[zl, :, core], w_.at[zl, :, core])
    vel_done = ring_z.exchange(lambda q: vsrc.at[q], vz.at[zh])
    vz[zh] = vsrc[zh]
    for c in loads[1:]:
        c.wait()
    q_done()

    def place(h):
        return (
            lax.div(h, GROUP),
            lax.rem(h, GROUP),
            pl.ds(pl.multiple_of(h * HDIM, HDIM), HDIM),
            pl.ds(pl.multiple_of(lax.rem(h, GROUP) * HDIM, HDIM), HDIM),
        )

    def over_heads(body):
        def step(n, carry):
            for k in range(PER_STEP):
                body(n * PER_STEP + k)
            return carry

        lax.fori_loop(0, HEADS // PER_STEP, step, 0)

    def scores(h):
        b, i, at, _ = place(h)
        q = qx[:, 0, :, at].reshape(128, HDIM)
        qt = qx[:, 1, :, at].reshape(128, HDIM)
        k = k_[:, at]
        score = mm(k, q, NT) * scale
        slope = (mm(k, qt, NT) + mm(kt_[:, at], q, NT)) * scale
        peak = jnp.max(score, axis=0, keepdims=True)
        expd = jnp.exp(score - peak)
        st[b, 0, pl.ds(i, 1), :] = peak
        st[b, 1, pl.ds(i, 1), :] = jnp.sum(expd, axis=0, keepdims=True)
        st[b, 2, pl.ds(i, 1), :] = jnp.sum(expd * slope, axis=0, keepdims=True)
        sc[h] = score
        sl[h] = slope

    over_heads(scores)

    def merged(parts):
        top = parts[0][0]
        for t in parts[1:]:
            top = jnp.maximum(top, t[0])
        w = [jnp.exp(t[0] - top) for t in parts]
        norm = sum(a * t[1] for a, t in zip(w, parts))
        bent = sum(a * t[2] for a, t in zip(w, parts))
        return top, norm, bent

    done = ring_x.exchange(lambda q: st.at[q], st_x.at[x])
    st_x[x] = st[x]
    done()
    top, norm, bent = merged([st_x[j] for j in range(4)])
    st_z[zh, 0] = top
    st_z[zh, 1] = norm
    st_z[zh, 2] = bent
    done = ring_z.exchange(lambda q: st_z.at[zh], st_z.at[zh])
    w_done()
    twin_copy = net.copy(w_.at[:, :, core], w_.at[:, :, core], twin)
    vel_done()
    vel_done = ring_x.exchange(lambda q: vz.at[:, q], vx.at[x])
    vx[x] = vz[:, x]
    done()
    top, norm, bent = merged([st_z[j] for j in range(4)])
    lm[x, 0] = top + jnp.log(norm)
    lm[x, 1] = bent / norm
    ring_x.exchange(lambda q: lm.at[x], lm.at[x])()

    def outputs(h):
        b, i, at, out = place(h)
        prob = jnp.exp(sc[h] - lm[b, 0, pl.ds(i, 1), :])
        mix = prob * (1.0 + gap * (sl[h] - lm[b, 1, pl.ds(i, 1), :]))
        sc[h] = prob
        part = mm(mix.astype(BF16), v_[:, at], TN) + mm((gap * prob).astype(BF16), vt_[:, at], TN)
        s_c[b, :, out] = part.astype(BF16)

    over_heads(outputs)

    def all_reduce(c, tx, lx, rx, z, tz, lz, rz, full):
        ring_x.scatter(c, rows_half(64), tx, lx, rx, rows_half1(64))
        t = c[x].astype(F32) + lx[...].astype(F32) + rx[...].astype(F32)
        z[...] = t.astype(BF16).reshape(4, 32, 640)
        ring_z.scatter(z, rows_half(16), tz, lz, rz, rows_half1(16))
        t = z[zh].astype(F32) + lz[...].astype(F32) + rz[...].astype(F32)
        full[x, zh] = t.astype(BF16)
        ring_z.gather(full, lambda buf, b, k: buf.at[x, b, pl.ds(16 * k, 16)])()
        ring_x.gather(full, lambda buf, b, k: buf.at[b, pl.ds(2 * k, 2)])()

    all_reduce(s_c, s_tx, s_lx, s_rx, s_z, s_tz, s_lz, s_rz, s_full)

    twin_copy.wait_recv()
    vel_done()
    u = -vx[...].reshape(128, 160)
    for b in range(4):
        u = u + mm(s_full[b].reshape(128, 640), w_[b].reshape(640, 160), NN)
    u = u.astype(BF16)
    for b in range(4):
        g_c[b] = mm(u, w_[b].reshape(640, 160), NT).astype(BF16)

    all_reduce(g_c, g_tx, g_lx, g_rx, g_z, g_tz, g_lz, g_rz, g_full)

    def values_back(h):
        b, i, at, out = place(h)
        go = g_full[b, :, :, out].reshape(128, HDIM)
        prob = sc[h]
        dprob = mm(v_[:, at], go, NT)
        dl[b, pl.ds(i, 1), :] = jnp.sum(prob * dprob, axis=0, keepdims=True)
        sl[h] = dprob
        dv_[:, at] = mm(prob.astype(BF16), go, NN).astype(BF16)

    over_heads(values_back)
    dv_store = pltpu.make_async_copy(dv_, dv_hbm.at[0], store_sem.at[0])
    dv_store.start()

    done = ring_x.exchange(lambda q: dl.at[q], dl_x.at[x])
    dl_x[x] = dl[x]
    done()
    dl_z[zh] = dl_x[0] + dl_x[1] + dl_x[2] + dl_x[3]
    ring_z.exchange(lambda q: dl_z.at[zh], dl_z.at[zh])()
    dm[x] = dl_z[0] + dl_z[1] + dl_z[2] + dl_z[3]
    ring_x.exchange(lambda q: dm.at[x], dm.at[x])()

    def keys_back(h):
        b, i, at, out = place(h)
        ds = (sc[h] * (sl[h] - dm[b, pl.ds(i, 1), :]) * scale).astype(BF16)
        dk_[:, at] = mm(ds, qx[:, 0, :, at].reshape(128, HDIM), NN).astype(BF16)
        a_c[:, :, at] = mm(ds, k_[:, at], TN).astype(BF16).reshape(4, 32, HDIM)

    over_heads(keys_back)
    dk_store = pltpu.make_async_copy(dk_, dk_hbm.at[0], store_sem.at[1])
    dk_store.start()

    ring_x.scatter(a_c, rows_half(16), a_tx, a_lx, a_rx, rows_half1(16))
    t = a_c[x].astype(F32) + a_lx[...].astype(F32) + a_rx[...].astype(F32)
    for z in range(4):
        r = t[8 * z : 8 * z + 8]
        a_z[z] = jnp.concatenate([r[:, :1280], r[:, 1280:]], axis=0).astype(BF16)
    cols = lambda buf, k: buf.at[:, pl.ds(640 * k, 640)]
    ring_z.scatter(
        a_z, lambda buf, b, k: buf.at[b, :, pl.ds(640 * k, 640)], a_tz, a_lz, a_rz, cols
    )
    t = a_z[zh].astype(F32) + a_lz[...].astype(F32) + a_rz[...].astype(F32)
    gq_out[0] = jnp.concatenate([t[:8], t[8:]], axis=1).astype(BF16)

    for c in net.all:
        c.wait_send()
    dv_store.wait()
    dk_store.wait()


def vm(*shape, dtype=BF16):
    return pltpu.VMEM(shape, dtype)


def reduce_scratch():
    return [
        vm(4, 128, 640), vm(2, 64, 640), vm(128, 640), vm(128, 640),
        vm(4, 32, 640), vm(2, 16, 640), vm(32, 640), vm(32, 640), vm(4, 4, 32, 640),
    ]


def local(queries, query_tangent, keys, values, key_tangent, value_tangent, velocity, out_weight, pair_index):
    vmem = pl.BlockSpec(memory_space=pltpu.VMEM)
    smem = pl.BlockSpec(memory_space=pltpu.SMEM)
    hbm = pl.BlockSpec(memory_space=pl.ANY)
    return tuple(
        pl.pallas_call(
            kernel,
            out_shape=[
                jax.ShapeDtypeStruct((1, 8, 2560), BF16),
                jax.ShapeDtypeStruct((1, 144, 2560), BF16),
                jax.ShapeDtypeStruct((1, 144, 2560), BF16),
            ],
            in_specs=[vmem, vmem, vmem, smem] + [hbm] * 5,
            out_specs=[vmem, hbm, hbm],
            scratch_shapes=[
                *[vm(144, 2560)] * 4,
                vm(4, 4, 2, 80, 160),
                *[vm(144, 2560)] * 2,
                vm(4, 16, 2560),
                vm(4, 2, 32, 2560),
                *[vm(4, 4, 8, 160, dtype=F32)] * 3,
                *[vm(HEADS, 144, 128, dtype=F32)] * 2,
                *[vm(4, 3, 8, 128, dtype=F32)] * 3,
                vm(4, 2, 8, 128, dtype=F32),
                *[vm(4, 8, 128, dtype=F32)] * 4,
                *reduce_scratch(),
                *reduce_scratch(),
                vm(4, 32, 2560), vm(2, 16, 2560), vm(32, 2560), vm(32, 2560),
                vm(4, 16, 1280), vm(2, 16, 640), vm(16, 1280), vm(16, 1280),
                pltpu.SemaphoreType.DMA((5,)),
                pltpu.SemaphoreType.DMA((2,)),
                pltpu.SemaphoreType.DMA((COPIES,)),
                pltpu.SemaphoreType.DMA((COPIES,)),
            ],
            compiler_params=pltpu.CompilerParams(
                collective_id=0, has_side_effects=True, vmem_limit_bytes=48 * 1024 * 1024
            ),
        )(
            queries, query_tangent, velocity, pair_index,
            keys, values, key_tangent, value_tangent, out_weight,
        )
    )


def solution(mesh):
    row = P("dp", "ctx", None)
    return jax.shard_map(
        local,
        mesh=mesh,
        in_specs=(row,) * 7 + (P("dp", "ctx"), P("dp", None)),
        out_specs=(row, row, row),
        check_vma=False,
    )
```
